32 devices in a mesh: row: 8 (over z, x), col: 4 (over y, core).
Axes of the slice: x: 2, y: 2, z: 4, core: 2. Of those that a mesh axis runs over, the one named last changes fastest.
Arguments:
- right_side: float32 [16, 512, 512], P(None, 'row', 'col'), may hold values from -8 to 8
- guess: float32 [16, 512, 512], P(None, 'row', 'col'), may hold values from -8 to 8
- material: int32 [16, 512, 512], P(None, 'row', 'col'), may hold values from 0 to 7
- conductivity: float32 [8], replicated, may hold values from 0.5 to 8
- capacity: float32 [8], replicated, may hold values from 0.004 to 0.1
Outputs:
- temperature: float32 [16, 512, 512], P(None, 'row', 'col')
- residual: float32 [16, 512, 512], P(None, 'row', 'col')
The draws below stay inside these ranges and needn't reach their ends.
All inputs are finite; a program needn't handle non-finite values.
Results may differ from the reference program's by a relative error of at most 0.000042.
Values sent between devices are 32-bit elements; how exact they have to be, the bound alone decides.
A program may use at most 64 MiB of HBM per device.

```python
import math
import jax
import jax.numpy as jnp

NZ = 16
COARSEN = 16
PRE = 2
POST = 2
CSWEEPS = 8
NCLASS = 8
NX = 512
NY = 512


def draw_material(key, part):
    key = jax.random.fold_in(key, 7)
    key_base = jax.random.fold_in(key, 1)
    key_other = jax.random.fold_in(key, 2)
    key_keep = jax.random.fold_in(key, 3)
    base = jax.random.randint(key_base, (NZ, NX // COARSEN, NY // COARSEN), 0, NCLASS)
    base_fine = jnp.repeat(jnp.repeat(base, COARSEN, axis=1), COARSEN, axis=2)
    other = jax.random.randint(key_other, (NZ, NX, NY), 0, NCLASS)
    keep = jax.random.randint(key_keep, (NZ, NX, NY), 0, 4) < 3
    return jnp.where(keep, base_fine, other).astype(jnp.int32)


def levels(stream_key, extent, cuts, least, high):
    def one(dim, parts):
        heights = jax.random.uniform(jax.random.fold_in(jax.random.fold_in(stream_key, 6), dim), (parts,), jnp.float32, least / len(cuts), high / len(cuts))
        return jnp.repeat(jnp.exp(heights), extent[dim] // parts).reshape((-1,) + (1,) * (len(extent) - dim - 1))

    level = one(*cuts[0])
    for cut in cuts[1:]:
        level = level * one(*cut)
    return level


def gaussian(key, dims, deviation, reach, pieces=(), held_as=jnp.bfloat16):
    loudness = levels(key, dims, pieces, -0.22, 0.18) if pieces else 1.0
    array = jax.random.normal(key, dims, jnp.float32) * deviation * loudness
    return jnp.minimum(jnp.maximum(array, -reach), reach).astype(held_as)


def setup_inputs(seed: int = 0) -> dict:
    key_of = jax.random.split(jax.random.key(seed), 6)
    return {
        "right_side": gaussian(key_of[0], (NZ, NX, NY), 1.0, 8.0, ((1, 8), (2, 4)), jnp.float32),
        "guess": gaussian(key_of[1], (NZ, NX, NY), 1.0, 8.0, ((1, 8), (2, 4)), jnp.float32),
        "material": draw_material(jax.random.fold_in(key_of[5], 71), 0),
        "conductivity": jnp.clip(jnp.exp(jax.random.uniform(key_of[3], (NCLASS,), jnp.float32, math.log(0.5), math.log(8.0))), 0.5, 8.0),
        "capacity": jnp.clip(jnp.exp(jax.random.uniform(key_of[4], (NCLASS,), jnp.float32, math.log(0.004), math.log(0.1))), 0.004, 0.1),
    }


OMEGA = 0.8


def shifted(padded):
    return [padded[2:, 1:-1, 1:-1], padded[:-2, 1:-1, 1:-1],
            padded[1:-1, 2:, 1:-1], padded[1:-1, :-2, 1:-1],
            padded[1:-1, 1:-1, 2:], padded[1:-1, 1:-1, :-2]]


def face_coefs(kap, zfactor):
    coefs = []
    for index, other in enumerate(shifted(jnp.pad(kap, 1))):
        coef = 0.5 * (kap + other)
        if index < 2:
            coef = coef * zfactor
        coefs.append(coef)
    return coefs


def fine_apply(field, coefs, cap):
    result = cap * field
    for coef, other in zip(coefs, shifted(jnp.pad(field, 1))):
        result = result + coef * (field - other)
    return result


def thomas(diag_line, upper, rhs):
    depth = rhs.shape[0]
    gains = []
    heads = []
    denom = diag_line[0]
    gains.append(upper[0] / denom)
    heads.append(rhs[0] / denom)
    for level in range(1, depth):
        denom = diag_line[level] - upper[level - 1] * gains[level - 1]
        gains.append(upper[level] / denom)
        heads.append((rhs[level] + upper[level - 1] * heads[level - 1]) / denom)
    values = [None] * depth
    values[depth - 1] = heads[depth - 1]
    for level in range(depth - 2, -1, -1):
        values[level] = heads[level] + gains[level] * values[level + 1]
    return jnp.stack(values, axis=0)


def reference(right_side, guess, material, conductivity, capacity):
    kappa = jnp.take(conductivity, material)
    cap = jnp.take(capacity, material)
    coefs = face_coefs(kappa, 1.0)
    diag = cap
    for coef in coefs:
        diag = diag + coef
    field = guess
    for sweep in range(PRE):
        field = field + OMEGA * (right_side - fine_apply(field, coefs, cap)) / diag
    fine_res = right_side - fine_apply(field, coefs, cap)
    depth, width_x, width_y = fine_res.shape
    shape_c = (depth, width_x // COARSEN, COARSEN, width_y // COARSEN, COARSEN)
    coarse_res = fine_res.reshape(shape_c).sum(axis=(2, 4))
    kbar = kappa.reshape(shape_c).sum(axis=(2, 4)) / (COARSEN * COARSEN)
    capc = cap.reshape(shape_c).sum(axis=(2, 4))
    ccoefs = face_coefs(kbar, float(COARSEN * COARSEN))
    dcoarse = capc
    for coef in ccoefs:
        dcoarse = dcoarse + coef
    upper = ccoefs[0].at[-1].set(0.0)
    correction = jnp.zeros_like(coarse_res)
    for sweep in range(CSWEEPS):
        others = shifted(jnp.pad(correction, 1))
        rhs = coarse_res
        for index in range(2, 6):
            rhs = rhs + ccoefs[index] * others[index]
        correction = thomas(dcoarse, upper, rhs)
    wide = jnp.broadcast_to(correction[:, :, None, :, None], shape_c).reshape(fine_res.shape)
    field = field + wide
    for sweep in range(POST):
        field = field + OMEGA * (right_side - fine_apply(field, coefs, cap)) / diag
    residual = right_side - fine_apply(field, coefs, cap)
    return field, residual
```

```python
import functools
import math

import jax
import jax.numpy as jnp
from jax import lax
from jax.experimental import pallas as pl
from jax.experimental.pallas import tpu as pltpu
from jax.sharding import PartitionSpec as P

COARSEN = 16
PRE = 2
POST = 2
CSWEEPS = 8
OMEGA = 0.8
HALO = 8
LANES = 128
HIGH = lax.Precision.HIGHEST
MESH = pl.DeviceIdType.MESH


def lane_ids(shape):
    return lax.broadcasted_iota(jnp.int32, shape, len(shape) - 1)


def row_ids(shape):
    return lax.broadcasted_iota(jnp.int32, shape, len(shape) - 2)


def kernel(
    sizes,
    cond_ref, capa_ref, rhs_ref, guess_ref, mat_ref,
    out_ref, res_ref,
    va, vb, kap, cap, cz, cx, cy, rx, wgt, dia,
    mhalo, pack_l, pack_r, recv_l, recv_r, kl, kr,
    xsum, tile_k, tile_r, grid_k, grid_r,
    hx, hy, hup, hinv, hgain, hback, hres, ecor,
    fsend, frecv, ksend, krecv, rsend, rrecv,
):
    nrow, ncol, reach_r, reach_c = sizes
    depth, wx, wy = rhs_ref.shape
    ext = wx + 2 * HALO
    cells_x = wx // COARSEN
    cells_y = wy // COARSEN
    nclass = cond_ref.shape[0]
    row = lax.axis_index("row")
    col = lax.axis_index("col")
    rows_c = grid_r.shape[1]

    def exists(dr, dc):
        ok = (row + dr >= 0) & (row + dr < nrow)
        return ok & (col + dc >= 0) & (col + dc < ncol)

    def device(dr, dc):
        return (lax.rem(row + dr + nrow, nrow), lax.rem(col + dc + ncol, ncol))

    peers = [
        (dr, dc)
        for dr in range(-reach_r, reach_r + 1)
        for dc in range(-reach_c, reach_c + 1)
        if (dr, dc) != (0, 0)
    ]

    grid_k[...] = jnp.zeros_like(grid_k)
    grid_r[...] = jnp.zeros_like(grid_r)
    mhalo[...] = jnp.zeros_like(mhalo)
    recv_l[...] = jnp.zeros_like(recv_l)
    recv_r[...] = jnp.zeros_like(recv_r)
    lo, hi = slice(0, HALO), slice(ext - HALO, ext)
    own = slice(HALO, HALO + wx)
    for side in (lo, hi):
        va[1 : depth + 1, side, :wy] = jnp.zeros((depth, HALO, wy), jnp.float32)
        rx[:, side, :wy] = jnp.zeros((depth, HALO, wy), jnp.float32)

    barrier = pltpu.get_barrier_semaphore()
    for dr, dc in peers:
        @pl.when(exists(dr, dc))
        def _():
            pl.semaphore_signal(barrier, inc=1, device_id=device(dr, dc), device_id_type=MESH)

    lane = lane_ids((wx, LANES))
    for index, source in enumerate((guess_ref, rhs_ref, mat_ref)):
        left = jnp.zeros((wx, LANES), jnp.float32)
        right = jnp.zeros((wx, LANES), jnp.float32)
        for z in range(depth):
            plane = source[z].astype(jnp.float32)
            here = lane // 8 == z
            left = jnp.where(here, pltpu.roll(plane, (8 * z) % LANES, 1), left)
            right = jnp.where(here, pltpu.roll(plane, (8 * z + 8) % LANES, 1), right)
        pack_l[index] = left
        pack_r[index] = right

    tall_p = jnp.minimum(row + reach_r, nrow - 1) - jnp.maximum(row - reach_r, 0) + 1
    wide_p = jnp.minimum(col + reach_c, ncol - 1) - jnp.maximum(col - reach_c, 0) + 1
    pl.semaphore_wait(barrier, tall_p * wide_p - 1)

    zs = slice(1, depth + 1)
    last = slice(wx - HALO, wx)
    first = slice(0, HALO)
    plan = []
    for dr, src, dst in ((1, last, lo), (-1, first, hi)):
        plan.append((dr, 0, guess_ref.at[:, src, :], va.at[zs, dst, 0:wy]))
        plan.append((dr, 0, rhs_ref.at[:, src, :], rx.at[:, dst, 0:wy]))
        plan.append((dr, 0, mat_ref.at[:, src, :], mhalo.at[0 if dr == 1 else 1]))
    for dc, pack, recv in ((1, pack_r, recv_l), (-1, pack_l, recv_r)):
        plan.append((0, dc, pack, recv.at[:, own, :]))
        plan.append((1, dc, pack.at[:, last, :], recv.at[:, lo, :]))
        plan.append((-1, dc, pack.at[:, first, :], recv.at[:, hi, :]))
    fine = []
    for index, (dr, dc, src, dst) in enumerate(plan):
        copy = pltpu.make_async_remote_copy(
            src_ref=src, dst_ref=dst, send_sem=fsend.at[index], recv_sem=frecv.at[index],
            device_id=device(dr, dc), device_id_type=MESH,
        )
        fine.append((dr, dc, copy))

    def start_all(copies):
        for dr, dc, copy in copies:
            @pl.when(exists(dr, dc))
            def _():
                copy.start()

    def recv_all(copies):
        for dr, dc, copy in copies:
            @pl.when(exists(-dr, -dc))
            def _():
                copy.wait_recv()

    def sent_all(copies):
        for dr, dc, copy in copies:
            @pl.when(exists(dr, dc))
            def _():
                copy.wait_send()

    start_all(fine)

    def lookup(classes):
        kval = jnp.full(classes.shape, cond_ref[0], jnp.float32)
        cval = jnp.full(classes.shape, capa_ref[0], jnp.float32)
        for k in range(1, nclass):
            hit = classes == k
            kval = jnp.where(hit, cond_ref[k], kval)
            cval = jnp.where(hit, capa_ref[k], cval)
        return kval, cval

    def xblocks(plane):
        part = plane.reshape(cells_x, COARSEN // 8, 8, wy).sum(axis=1)
        return part.sum(axis=1)

    xsum[...] = jnp.zeros_like(xsum)

    def own_fields(z, carry):
        kval, cval = lookup(mat_ref[z])
        kap[z + 1, own, 0:wy] = kval
        cap[z, own, 0:wy] = cval
        rx[z, own, 0:wy] = rhs_ref[z]
        va[z + 1, own, 0:wy] = guess_ref[z]
        xsum[0, z, 0:cells_x, :] = xblocks(kval)
        xsum[1, z, 0:cells_x, :] = xblocks(cval)
        return carry

    lax.fori_loop(0, depth, own_fields, 0)

    gather_rows = lax.broadcasted_iota(jnp.int32, (wy, LANES), 0) // COARSEN
    summing = (gather_rows == lane_ids((wy, LANES)) % cells_y).astype(jnp.float32)
    zshape = (depth, 8, LANES)
    zmask = lane_ids(zshape) // cells_y == lax.broadcasted_iota(jnp.int32, zshape, 0)

    def coarse_tile(which):
        block = jnp.dot(xsum[which].reshape(depth * 8, wy), summing, precision=HIGH,
                        preferred_element_type=jnp.float32)
        return jnp.where(zmask, block.reshape(zshape), 0.0).sum(axis=0)[0:cells_x]

    def spread(tile, grid, sends, recvs):
        copies = []
        for index, (dr, dc) in enumerate(peers):
            at = cells_x * (reach_r - dr)
            copy = pltpu.make_async_remote_copy(
                src_ref=tile, dst_ref=grid.at[:, reach_c - dc, at : at + cells_x, :],
                send_sem=sends.at[index], recv_sem=recvs.at[index],
                device_id=device(dr, dc), device_id_type=MESH,
            )
            copies.append((dr, dc, copy))
        return copies

    mid = slice(cells_x * reach_r, cells_x * (reach_r + 1))
    gk = grid_k
    tile_k[0] = coarse_tile(0) * (1.0 / (COARSEN * COARSEN))
    tile_k[1] = coarse_tile(1)
    spread_k = spread(tile_k, gk, ksend, krecv)
    start_all(spread_k)
    gk[0, reach_c, mid, :] = tile_k[0]
    gk[1, reach_c, mid, :] = tile_k[1]

    recv_all(fine)
    for field, side_ok in ((0, exists(-1, 0)), (1, exists(1, 0))):
        at = lo if field == 0 else hi
        kval, cval = lookup(mhalo[field])
        kap[zs, at, 0:wy] = jnp.where(side_ok, kval, 0.0)
        cap[:, at, 0:wy] = jnp.where(side_ok, cval, 0.0)
    prow = row_ids((ext, LANES))
    rows_ok = ((prow >= HALO) | (row > 0)) & ((prow < ext - HALO) | (row < nrow - 1))
    for recv, keep, side_ok in ((recv_l, kl, col > 0), (recv_r, kr, col < ncol - 1)):
        kval, cval = lookup(recv[2].astype(jnp.int32))
        ok = rows_ok & side_ok
        keep[0] = jnp.where(ok, kval, 0.0)
        keep[1] = jnp.where(ok, cval, 0.0)
    elane = lane_ids((ext, LANES))
    rim = slice(wy, wy + LANES)
    for left, right, dst, first_z in (
        (kl.at[0], kr.at[0], kap, 1),
        (kl.at[1], kr.at[1], cap, 0),
        (recv_l.at[0], recv_r.at[0], va, 1),
        (recv_l.at[1], recv_r.at[1], rx, 0),
    ):
        lvals, rvals = left[...], right[...]
        for z in range(depth):
            shift = (LANES - 8 * z) % LANES
            a = pltpu.roll(rvals, shift, 1) if shift else rvals
            shift = (LANES - 8 - 8 * z) % LANES
            b = pltpu.roll(lvals, shift, 1) if shift else lvals
            dst[z + first_z, :, rim] = jnp.where(elane < 8, a, jnp.where(elane >= LANES - 8, b, 0.0))
    zero = jnp.zeros((ext, wy + LANES), jnp.float32)
    for field in (va, vb, kap):
        field[0] = zero
        field[depth + 1] = zero

    wide = wy + LANES

    def xnext(p):
        return pltpu.roll(p, ext - 1, 0)

    def xprev(p):
        return pltpu.roll(p, 1, 0)

    def ynext(p):
        return pltpu.roll(p, wide - 1, 1)

    def yprev(p):
        return pltpu.roll(p, 1, 1)

    cz[0] = 0.5 * kap[1]

    def coefs(z, carry):
        k = kap[z + 1]
        zc = 0.5 * (k + kap[z + 2])
        xc = 0.5 * (k + xnext(k))
        yc = 0.5 * (k + ynext(k))
        cz[z + 1] = zc
        cx[z] = xc
        cy[z] = yc
        d = cap[z] + zc
        d = d + cz[z]
        d = d + xc
        d = d + xprev(xc)
        d = d + yc
        d = d + yprev(yc)
        dia[z] = d
        wgt[z] = jnp.where(k > 0.0, OMEGA / d, 0.0)
        return carry

    lax.fori_loop(0, depth, coefs, 0)

    def around(src, z, v):
        t = rx[z] + cz[z + 1] * src[z + 2]
        t = t + cz[z] * src[z]
        xc = cx[z]
        t = t + xc * xnext(v)
        t = t + xprev(xc * v)
        yc = cy[z]
        t = t + yc * ynext(v)
        return t + yprev(yc * v)

    def clean(z, carry):
        va[z + 1] = jnp.where(kap[z + 1] > 0.0, va[z + 1], 0.0)
        return carry

    lax.fori_loop(0, depth, clean, 0)

    def sweep(src, dst):
        def body(z, carry):
            v = src[z + 1]
            dst[z + 1] = (1.0 - OMEGA) * v + wgt[z] * around(src, z, v)
            return carry

        lax.fori_loop(0, depth, body, 0)

    def inner_residual(src, z):
        v = src[z + 1]
        return (around(src, z, v) - dia[z] * v)[own, 0:wy]

    bufs = [va, vb]
    for _ in range(PRE):
        sweep(bufs[0], bufs[1])
        bufs.reverse()

    def restrict(z, carry):
        xsum[0, z, 0:cells_x, :] = xblocks(inner_residual(bufs[0], z))
        return carry

    lax.fori_loop(0, depth, restrict, 0)
    tile_r[0] = coarse_tile(0)
    spread_r = spread(tile_r, grid_r, rsend, rrecv)
    start_all(spread_r)
    grid_r[0, reach_c, mid, :] = tile_r[0]

    recv_all(spread_k)
    rows_w = grid_r.shape[2]
    wlane = lane_ids((rows_w, LANES))
    wrow = row_ids((rows_w, LANES))
    ncells_c = 2 * reach_c + 1
    crow = wrow + (row - reach_r) * cells_x
    ccol = wlane + (col - reach_c) * cells_y
    inside = (crow >= 0) & (crow < nrow * cells_x) & (ccol >= 0) & (ccol < ncol * cells_y)
    inside = inside & (wrow < (2 * reach_r + 1) * cells_x) & (wlane < ncells_c * cells_y)

    def window(grid, which, z):
        acc = jnp.zeros((rows_w, LANES), jnp.float32)
        for block in range(ncells_c):
            shift = (cells_y * (block - z)) % LANES
            part = grid[which, block]
            part = pltpu.roll(part, shift, 1) if shift else part
            acc = jnp.where(wlane // cells_y == block, part, acc)
        return jnp.where(inside, acc, 0.0)

    kb = [window(gk, 0, z) for z in range(depth)]
    factor = 0.5 * COARSEN * COARSEN
    below = factor * kb[0]
    gain = None
    for z in range(depth):
        k = kb[z]
        above = factor * (k + kb[z + 1]) if z + 1 < depth else factor * k
        xc = 0.5 * (k + pltpu.roll(k, rows_w - 1, 0))
        yc = 0.5 * (k + pltpu.roll(k, LANES - 1, 1))
        xm = pltpu.roll(xc, 1, 0)
        ym = pltpu.roll(yc, 1, 1)
        d = window(gk, 1, z) + above
        d = d + below
        d = d + xc
        d = d + xm
        d = d + yc
        d = d + ym
        upper = above if z + 1 < depth else jnp.zeros_like(above)
        denom = d if z == 0 else d - below * gain
        inv = jnp.where(inside, 1.0 / denom, 0.0)
        gain = upper * inv
        hx[z] = xc
        hy[z] = yc
        hinv[z] = inv
        hgain[z] = gain
        hback[z] = below * inv if z else jnp.zeros_like(inv)
        below = above

    recv_all(spread_r)
    for z in range(depth):
        hres[z] = window(grid_r, 0, z)
        ecor[z] = jnp.zeros((rows_w, LANES), jnp.float32)

    def coarse_sweep(step, carry):
        head = None
        heads = []
        for z in range(depth):
            e = ecor[z]
            xc, yc = hx[z], hy[z]
            r = hres[z] + xc * pltpu.roll(e, rows_w - 1, 0)
            r = r + pltpu.roll(xc * e, 1, 0)
            r = r + yc * pltpu.roll(e, LANES - 1, 1)
            r = r + pltpu.roll(yc * e, 1, 1)
            r = r * hinv[z]
            head = r if z == 0 else r + hback[z] * head
            heads.append(head)
        value = heads[-1]
        ecor[depth - 1] = value
        for z in range(depth - 2, -1, -1):
            value = heads[z] + hgain[z] * value
            ecor[z] = value
        return carry

    lax.fori_loop(0, CSWEEPS, coarse_sweep, 0)

    own_r = cells_x * reach_r
    low_r = (own_r - 1) // 8 * 8
    top_r = -(-(own_r + cells_x + 1) // 8) * 8
    ylane = lane_ids((LANES, wide))
    place = jnp.where(ylane < wy + LANES // 2, ylane // COARSEN, -1) + cells_y * reach_c
    picking = (lax.broadcasted_iota(jnp.int32, (LANES, wide), 0) == place).astype(jnp.float32)

    def prolong(z, carry):
        e = ecor[z, low_r:top_r, :]
        spread_y = jnp.dot(e, picking, precision=HIGH, preferred_element_type=jnp.float32)
        parts = []
        for cell in range(-1, cells_x + 1):
            at = own_r + cell - low_r
            tall = COARSEN if 0 <= cell < cells_x else HALO
            parts.append(jnp.broadcast_to(spread_y[at : at + 1, :], (tall, wide)))
        whole = jnp.concatenate(parts, axis=0)
        bufs[0][z + 1] = jnp.where(kap[z + 1] > 0.0, bufs[0][z + 1] + whole, 0.0)
        return carry

    lax.fori_loop(0, depth, prolong, 0)
    for _ in range(POST):
        sweep(bufs[0], bufs[1])
        bufs.reverse()

    def finish(z, carry):
        out_ref[z] = bufs[0][z + 1, own, 0:wy]
        res_ref[z] = inner_residual(bufs[0], z)
        return carry

    lax.fori_loop(0, depth, finish, 0)
    sent_all(fine)
    sent_all(spread_k)
    sent_all(spread_r)


def shards(nrow, ncol, right_side, guess, material, conductivity, capacity):
    depth, wx, wy = right_side.shape
    ext, wide = wx + 2 * HALO, wy + LANES
    cells_x, cells_y = wx // COARSEN, wy // COARSEN
    reach_r = min(math.ceil((CSWEEPS + 1) / cells_x), nrow - 1)
    reach_c = min(math.ceil((CSWEEPS + 1) / cells_y), ncol - 1)
    npeers = (2 * reach_r + 1) * (2 * reach_c + 1) - 1
    rows_w = -(-(2 * reach_r + 1) * cells_x // 8) * 8
    f32 = jnp.float32
    full = lambda planes: pltpu.VMEM((planes, ext, wide), f32)
    coarse = pltpu.VMEM((depth, rows_w, LANES), f32)
    dma = pltpu.SemaphoreType.DMA
    vmem = pl.BlockSpec(memory_space=pltpu.VMEM)
    smem = pl.BlockSpec(memory_space=pltpu.SMEM)
    shape = jax.ShapeDtypeStruct(right_side.shape, f32)
    return pl.pallas_call(
        functools.partial(kernel, (nrow, ncol, reach_r, reach_c)),
        out_shape=(shape, shape),
        in_specs=[smem, smem, vmem, vmem, vmem],
        out_specs=(vmem, vmem),
        scratch_shapes=[
            full(depth + 2), full(depth + 2), full(depth + 2), full(depth), full(depth + 1),
            full(depth), full(depth), full(depth), full(depth), full(depth),
            pltpu.VMEM((2, depth, HALO, wy), jnp.int32),
            pltpu.VMEM((3, wx, LANES), f32), pltpu.VMEM((3, wx, LANES), f32),
            pltpu.VMEM((3, ext, LANES), f32), pltpu.VMEM((3, ext, LANES), f32),
            pltpu.VMEM((2, ext, LANES), f32), pltpu.VMEM((2, ext, LANES), f32),
            pltpu.VMEM((2, depth, 8, wy), f32),
            pltpu.VMEM((2, cells_x, LANES), f32), pltpu.VMEM((1, cells_x, LANES), f32),
            pltpu.VMEM((2, 2 * reach_c + 1, rows_w, LANES), f32),
            pltpu.VMEM((1, 2 * reach_c + 1, rows_w, LANES), f32),
            coarse, coarse, coarse, coarse, coarse, coarse, coarse, coarse,
            dma((12,)), dma((12,)),
            dma((npeers,)), dma((npeers,)), dma((npeers,)), dma((npeers,)),
        ],
        compiler_params=pltpu.CompilerParams(
            collective_id=0, has_side_effects=True, vmem_limit_bytes=48 * 1024 * 1024
        ),
    )(conductivity, capacity, right_side, guess, material)


def solution(mesh):
    placed = (P(None, "row", "col"), P(None, "row", "col"), P(None, "row", "col"), P(), P())
    return jax.shard_map(
        functools.partial(shards, mesh.shape["row"], mesh.shape["col"]),
        mesh=mesh,
        in_specs=placed,
        out_specs=(P(None, "row", "col"), P(None, "row", "col")),
        check_vma=False,
    )
```

```python
import functools
import math

import jax
import jax.numpy as jnp
from jax import lax
from jax.experimental import pallas as pl
from jax.experimental.pallas import tpu as pltpu
from jax.sharding import PartitionSpec as P

COARSEN = 16
PRE = 2
POST = 2
CSWEEPS = 8
OMEGA = 0.8
HALO = 8
LANES = 128
HIGH = lax.Precision.HIGHEST
MESH = pl.DeviceIdType.MESH


def lane_ids(shape):
    return lax.broadcasted_iota(jnp.int32, shape, len(shape) - 1)


def row_ids(shape):
    return lax.broadcasted_iota(jnp.int32, shape, len(shape) - 2)


def kernel(
    sizes,
    cond_in, capa_in, rhs_in, guess_in, mat_in,
    out_ref, res_ref,
    cond_ref, capa_ref, rhs_ref, guess_ref, mat_ref, isem,
    va, vb, kap, cap, cz, cx, cy, rx, wgt, dia,
    uhalo, upack_l, upack_r, ur_l, ur_r, mhalo, pack_l, pack_r, recv_l, recv_r, kl, kr,
    xsum, tile_k, tile_r, grid_k, grid_r,
    hx, hy, hup, hinv, hgain, hback, hres, ecor,
    fsend, frecv, usend, urecv, ksend, krecv, rsend, rrecv,
):
    nrow, ncol, reach_r, reach_c = sizes
    depth, wx, wy = rhs_ref.shape
    ext = wx + 2 * HALO
    cells_x = wx // COARSEN
    cells_y = wy // COARSEN
    nclass = cond_ref.shape[0]
    row = lax.axis_index("row")
    col = lax.axis_index("col")
    rows_c = grid_r.shape[1]

    def exists(dr, dc):
        ok = (row + dr >= 0) & (row + dr < nrow)
        return ok & (col + dc >= 0) & (col + dc < ncol)

    def device(dr, dc):
        return (lax.rem(row + dr + nrow, nrow), lax.rem(col + dc + ncol, ncol))

    peers = [
        (dr, dc)
        for dr in range(-reach_r, reach_r + 1)
        for dc in range(-reach_c, reach_c + 1)
        if (dr, dc) != (0, 0)
    ]

    local = [
        pltpu.make_async_copy(src, dst, isem.at[index])
        for index, (src, dst) in enumerate((
            (guess_in, guess_ref), (rhs_in, rhs_ref), (mat_in, mat_ref),
            (cond_in, cond_ref), (capa_in, capa_ref),
        ))
    ]
    for copy in local:
        copy.start()
    uhalo[...] = jnp.zeros_like(uhalo)
    ur_l[...] = jnp.zeros_like(ur_l)
    ur_r[...] = jnp.zeros_like(ur_r)
    grid_k[...] = jnp.zeros_like(grid_k)
    grid_r[...] = jnp.zeros_like(grid_r)
    mhalo[...] = jnp.zeros_like(mhalo)
    recv_l[...] = jnp.zeros_like(recv_l)
    recv_r[...] = jnp.zeros_like(recv_r)
    lo, hi = slice(0, HALO), slice(ext - HALO, ext)
    own = slice(HALO, HALO + wx)
    for side in (lo, hi):
        va[1 : depth + 1, side, :wy] = jnp.zeros((depth, HALO, wy), jnp.float32)
        rx[:, side, :wy] = jnp.zeros((depth, HALO, wy), jnp.float32)

    barrier = pltpu.get_barrier_semaphore()
    for dr, dc in peers:
        @pl.when(exists(dr, dc))
        def _():
            pl.semaphore_signal(barrier, inc=1, device_id=device(dr, dc), device_id_type=MESH)

    lane = lane_ids((wx, LANES))

    def packed(plane_of):
        left = jnp.zeros((wx, LANES), jnp.float32)
        right = jnp.zeros((wx, LANES), jnp.float32)
        for z in range(depth):
            plane = plane_of(z)
            here = lane // 8 == z
            left = jnp.where(here, pltpu.roll(plane, (8 * z) % LANES, 1), left)
            right = jnp.where(here, pltpu.roll(plane, (8 * z + 8) % LANES, 1), right)
        return left, right

    for copy in local:
        copy.wait()
    for index, source in enumerate((guess_ref, rhs_ref, mat_ref)):
        left, right = packed(lambda z: source[z].astype(jnp.float32))
        pack_l[index] = left
        pack_r[index] = right

    tall_p = jnp.minimum(row + reach_r, nrow - 1) - jnp.maximum(row - reach_r, 0) + 1
    wide_p = jnp.minimum(col + reach_c, ncol - 1) - jnp.maximum(col - reach_c, 0) + 1
    pl.semaphore_wait(barrier, tall_p * wide_p - 1)

    zs = slice(1, depth + 1)

    def edge(dr, width):
        if dr == 1:
            return slice(wx - width, wx), slice(HALO - width, HALO)
        return slice(0, width), slice(HALO + wx, HALO + wx + width)

    def remote(plan, sends, recvs):
        copies = []
        for index, (dr, dc, src, dst) in enumerate(plan):
            copy = pltpu.make_async_remote_copy(
                src_ref=src, dst_ref=dst, send_sem=sends.at[index], recv_sem=recvs.at[index],
                device_id=device(dr, dc), device_id_type=MESH,
            )
            copies.append((dr, dc, copy))
        return copies

    def strips(packs, recvs, middle, wide_of):
        plan = []
        for dc, pack, recv in ((1, packs[1], recvs[0]), (-1, packs[0], recvs[1])):
            plan.append((0, dc, pack, recv.at[middle + (own,)]))
            for dr in (1, -1):
                src, dst = edge(dr, wide_of)
                plan.append((dr, dc, pack.at[middle + (src,)], recv.at[middle + (dst,)]))
        return plan

    near = PRE + 1
    plan = []
    for dr in (1, -1):
        src, dst = edge(dr, near)
        thin_src, thin_dst = edge(dr, near - 1)
        shift = 0 if dr == 1 else HALO + wx
        in_halo = slice(dst.start - shift, dst.stop - shift)
        plan.append((dr, 0, guess_ref.at[:, src, :], va.at[zs, dst, 0:wy]))
        plan.append((dr, 0, mat_ref.at[:, src, :], mhalo.at[0 if dr == 1 else 1, :, in_halo, :]))
        plan.append((dr, 0, rhs_ref.at[:, thin_src, :], rx.at[:, thin_dst, 0:wy]))
    plan += strips((pack_l, pack_r), (recv_l, recv_r), (slice(None),), near)
    fine = remote(plan, fsend, frecv)
    plan = []
    for dr in (1, -1):
        src, dst = edge(dr, POST + 1)
        shift = 0 if dr == 1 else HALO + wx
        src = slice(src.start + HALO, src.stop + HALO)
        in_halo = slice(dst.start - shift, dst.stop - shift)
        held = va if PRE % 2 == 0 else vb
        plan.append((dr, 0, held.at[zs, src, 0:wy], uhalo.at[0 if dr == 1 else 1, :, in_halo, :]))
    plan += strips((upack_l, upack_r), (ur_l, ur_r), (), POST + 1)
    pre_edges = remote(plan, usend, urecv)

    def start_all(copies):
        for dr, dc, copy in copies:
            @pl.when(exists(dr, dc))
            def _():
                copy.start()

    def recv_all(copies):
        for dr, dc, copy in copies:
            @pl.when(exists(-dr, -dc))
            def _():
                copy.wait_recv()

    def sent_all(copies):
        for dr, dc, copy in copies:
            @pl.when(exists(dr, dc))
            def _():
                copy.wait_send()

    start_all(fine)

    def lookup(classes):
        kval = jnp.full(classes.shape, cond_ref[0], jnp.float32)
        cval = jnp.full(classes.shape, capa_ref[0], jnp.float32)
        for k in range(1, nclass):
            hit = classes == k
            kval = jnp.where(hit, cond_ref[k], kval)
            cval = jnp.where(hit, capa_ref[k], cval)
        return kval, cval

    def xblocks(plane):
        part = plane.reshape(cells_x, COARSEN // 8, 8, wy).sum(axis=1)
        return part.sum(axis=1)

    xsum[...] = jnp.zeros_like(xsum)

    def own_fields(z, carry):
        kval, cval = lookup(mat_ref[z])
        kap[z + 1, own, 0:wy] = kval
        cap[z, own, 0:wy] = cval
        rx[z, own, 0:wy] = rhs_ref[z]
        va[z + 1, own, 0:wy] = guess_ref[z]
        xsum[0, z, 0:cells_x, :] = xblocks(kval)
        xsum[1, z, 0:cells_x, :] = xblocks(cval)
        return carry

    lax.fori_loop(0, depth, own_fields, 0)

    gather_rows = lax.broadcasted_iota(jnp.int32, (wy, LANES), 0) // COARSEN
    summing = (gather_rows == lane_ids((wy, LANES)) % cells_y).astype(jnp.float32)
    zshape = (depth, 8, LANES)
    zmask = lane_ids(zshape) // cells_y == lax.broadcasted_iota(jnp.int32, zshape, 0)

    def coarse_tile(which):
        block = jnp.dot(xsum[which].reshape(depth * 8, wy), summing, precision=HIGH,
                        preferred_element_type=jnp.float32)
        return jnp.where(zmask, block.reshape(zshape), 0.0).sum(axis=0)[0:cells_x]

    def spread(tile, grid, sends, recvs):
        copies = []
        for index, (dr, dc) in enumerate(peers):
            at = cells_x * (reach_r - dr)
            copy = pltpu.make_async_remote_copy(
                src_ref=tile, dst_ref=grid.at[:, reach_c - dc, at : at + cells_x, :],
                send_sem=sends.at[index], recv_sem=recvs.at[index],
                device_id=device(dr, dc), device_id_type=MESH,
            )
            copies.append((dr, dc, copy))
        return copies

    mid = slice(cells_x * reach_r, cells_x * (reach_r + 1))
    gk = grid_k
    tile_k[0] = coarse_tile(0) * (1.0 / (COARSEN * COARSEN))
    tile_k[1] = coarse_tile(1)
    spread_k = spread(tile_k, gk, ksend, krecv)
    start_all(spread_k)
    gk[0, reach_c, mid, :] = tile_k[0]
    gk[1, reach_c, mid, :] = tile_k[1]

    recv_all(fine)
    for field, side_ok in ((0, exists(-1, 0)), (1, exists(1, 0))):
        at = lo if field == 0 else hi
        kval, cval = lookup(mhalo[field])
        kap[zs, at, 0:wy] = jnp.where(side_ok, kval, 0.0)
        cap[:, at, 0:wy] = jnp.where(side_ok, cval, 0.0)
    prow = row_ids((ext, LANES))
    rows_ok = ((prow >= HALO) | (row > 0)) & ((prow < ext - HALO) | (row < nrow - 1))
    for recv, keep, side_ok in ((recv_l, kl, col > 0), (recv_r, kr, col < ncol - 1)):
        kval, cval = lookup(recv[2].astype(jnp.int32))
        ok = rows_ok & side_ok
        keep[0] = jnp.where(ok, kval, 0.0)
        keep[1] = jnp.where(ok, cval, 0.0)
    elane = lane_ids((ext, LANES))
    rim = slice(wy, wy + LANES)

    def unpack(lvals, rvals, dst, first_z):
        for z in range(depth):
            shift = (LANES - 8 * z) % LANES
            a = pltpu.roll(rvals, shift, 1) if shift else rvals
            shift = (LANES - 8 - 8 * z) % LANES
            b = pltpu.roll(lvals, shift, 1) if shift else lvals
            dst[z + first_z, :, rim] = jnp.where(elane < 8, a, jnp.where(elane >= LANES - 8, b, 0.0))

    for left, right, dst, first_z in (
        (kl.at[0], kr.at[0], kap, 1),
        (kl.at[1], kr.at[1], cap, 0),
        (recv_l.at[0], recv_r.at[0], va, 1),
        (recv_l.at[1], recv_r.at[1], rx, 0),
    ):
        unpack(left[...], right[...], dst, first_z)
    zero = jnp.zeros((ext, wy + LANES), jnp.float32)
    for field in (va, vb, kap):
        field[0] = zero
        field[depth + 1] = zero

    wide = wy + LANES

    def xnext(p):
        return pltpu.roll(p, ext - 1, 0)

    def xprev(p):
        return pltpu.roll(p, 1, 0)

    def ynext(p):
        return pltpu.roll(p, wide - 1, 1)

    def yprev(p):
        return pltpu.roll(p, 1, 1)

    cz[0] = 0.5 * kap[1]

    def coefs(z, carry):
        k = kap[z + 1]
        zc = 0.5 * (k + kap[z + 2])
        xc = 0.5 * (k + xnext(k))
        yc = 0.5 * (k + ynext(k))
        cz[z + 1] = zc
        cx[z] = xc
        cy[z] = yc
        d = cap[z] + zc
        d = d + cz[z]
        d = d + xc
        d = d + xprev(xc)
        d = d + yc
        d = d + yprev(yc)
        dia[z] = d
        wgt[z] = jnp.where(k > 0.0, OMEGA / d, 0.0)
        return carry

    lax.fori_loop(0, depth, coefs, 0)

    def around(src, z, v):
        t = rx[z] + cz[z + 1] * src[z + 2]
        t = t + cz[z] * src[z]
        xc = cx[z]
        t = t + xc * xnext(v)
        t = t + xprev(xc * v)
        yc = cy[z]
        t = t + yc * ynext(v)
        return t + yprev(yc * v)

    def clean(z, carry):
        va[z + 1] = jnp.where(kap[z + 1] > 0.0, va[z + 1], 0.0)
        return carry

    lax.fori_loop(0, depth, clean, 0)

    def sweep(src, dst):
        def body(z, carry):
            v = src[z + 1]
            dst[z + 1] = (1.0 - OMEGA) * v + wgt[z] * around(src, z, v)
            return carry

        lax.fori_loop(0, depth, body, 0)

    def inner_residual(src, z):
        v = src[z + 1]
        return (around(src, z, v) - dia[z] * v)[own, 0:wy]

    bufs = [va, vb]
    for _ in range(PRE):
        sweep(bufs[0], bufs[1])
        bufs.reverse()

    def restrict(z, carry):
        xsum[0, z, 0:cells_x, :] = xblocks(inner_residual(bufs[0], z))
        return carry

    lax.fori_loop(0, depth, restrict, 0)
    tile_r[0] = coarse_tile(0)
    spread_r = spread(tile_r, grid_r, rsend, rrecv)
    start_all(spread_r)
    grid_r[0, reach_c, mid, :] = tile_r[0]
    upack_l[...], upack_r[...] = packed(lambda z: bufs[0][z + 1, own, 0:wy])
    start_all(pre_edges)

    recv_all(spread_k)
    rows_w = grid_r.shape[2]
    wlane = lane_ids((rows_w, LANES))
    wrow = row_ids((rows_w, LANES))
    ncells_c = 2 * reach_c + 1
    crow = wrow + (row - reach_r) * cells_x
    ccol = wlane + (col - reach_c) * cells_y
    inside = (crow >= 0) & (crow < nrow * cells_x) & (ccol >= 0) & (ccol < ncol * cells_y)
    inside = inside & (wrow < (2 * reach_r + 1) * cells_x) & (wlane < ncells_c * cells_y)

    def window(grid, which, z):
        acc = jnp.zeros((rows_w, LANES), jnp.float32)
        for block in range(ncells_c):
            shift = (cells_y * (block - z)) % LANES
            part = grid[which, block]
            part = pltpu.roll(part, shift, 1) if shift else part
            acc = jnp.where(wlane // cells_y == block, part, acc)
        return jnp.where(inside, acc, 0.0)

    kb = [window(gk, 0, z) for z in range(depth)]
    factor = 0.5 * COARSEN * COARSEN
    below = factor * kb[0]
    gain = None
    for z in range(depth):
        k = kb[z]
        above = factor * (k + kb[z + 1]) if z + 1 < depth else factor * k
        xc = 0.5 * (k + pltpu.roll(k, rows_w - 1, 0))
        yc = 0.5 * (k + pltpu.roll(k, LANES - 1, 1))
        xm = pltpu.roll(xc, 1, 0)
        ym = pltpu.roll(yc, 1, 1)
        d = window(gk, 1, z) + above
        d = d + below
        d = d + xc
        d = d + xm
        d = d + yc
        d = d + ym
        upper = above if z + 1 < depth else jnp.zeros_like(above)
        denom = d if z == 0 else d - below * gain
        inv = jnp.where(inside, 1.0 / denom, 0.0)
        gain = upper * inv
        hx[z] = xc
        hy[z] = yc
        hinv[z] = inv
        hgain[z] = gain
        hback[z] = below * inv if z else jnp.zeros_like(inv)
        below = above

    recv_all(spread_r)
    for z in range(depth):
        hres[z] = window(grid_r, 0, z)
        ecor[z] = jnp.zeros((rows_w, LANES), jnp.float32)

    def coarse_sweep(step, carry):
        head = None
        heads = []
        for z in range(depth):
            e = ecor[z]
            xc, yc = hx[z], hy[z]
            r = hres[z] + xc * pltpu.roll(e, rows_w - 1, 0)
            r = r + pltpu.roll(xc * e, 1, 0)
            r = r + yc * pltpu.roll(e, LANES - 1, 1)
            r = r + pltpu.roll(yc * e, 1, 1)
            r = r * hinv[z]
            head = r if z == 0 else r + hback[z] * head
            heads.append(head)
        value = heads[-1]
        ecor[depth - 1] = value
        for z in range(depth - 2, -1, -1):
            value = heads[z] + hgain[z] * value
            ecor[z] = value
        return carry

    lax.fori_loop(0, CSWEEPS, coarse_sweep, 0)

    recv_all(pre_edges)
    sent_all(pre_edges)
    bufs[0][zs, lo, 0:wy] = uhalo[0]
    bufs[0][zs, hi, 0:wy] = uhalo[1]
    unpack(ur_l[...], ur_r[...], bufs[0], 1)
    own_r = cells_x * reach_r
    low_r = (own_r - 1) // 8 * 8
    top_r = -(-(own_r + cells_x + 1) // 8) * 8
    ylane = lane_ids((LANES, wide))
    place = jnp.where(ylane < wy + LANES // 2, ylane // COARSEN, -1) + cells_y * reach_c
    picking = (lax.broadcasted_iota(jnp.int32, (LANES, wide), 0) == place).astype(jnp.float32)

    def prolong(z, carry):
        e = ecor[z, low_r:top_r, :]
        spread_y = jnp.dot(e, picking, precision=HIGH, preferred_element_type=jnp.float32)
        parts = []
        for cell in range(-1, cells_x + 1):
            at = own_r + cell - low_r
            tall = COARSEN if 0 <= cell < cells_x else HALO
            parts.append(jnp.broadcast_to(spread_y[at : at + 1, :], (tall, wide)))
        whole = jnp.concatenate(parts, axis=0)
        bufs[0][z + 1] = jnp.where(kap[z + 1] > 0.0, bufs[0][z + 1] + whole, 0.0)
        return carry

    lax.fori_loop(0, depth, prolong, 0)
    for _ in range(POST):
        sweep(bufs[0], bufs[1])
        bufs.reverse()

    def finish(z, carry):
        out_ref[z] = bufs[0][z + 1, own, 0:wy]
        res_ref[z] = inner_residual(bufs[0], z)
        return carry

    lax.fori_loop(0, depth, finish, 0)
    sent_all(fine)
    sent_all(spread_k)
    sent_all(spread_r)


def shards(nrow, ncol, right_side, guess, material, conductivity, capacity):
    depth, wx, wy = right_side.shape
    ext, wide = wx + 2 * HALO, wy + LANES
    cells_x, cells_y = wx // COARSEN, wy // COARSEN
    reach_r = min(math.ceil((CSWEEPS + 1) / cells_x), nrow - 1)
    reach_c = min(math.ceil((CSWEEPS + 1) / cells_y), ncol - 1)
    npeers = (2 * reach_r + 1) * (2 * reach_c + 1) - 1
    rows_w = -(-(2 * reach_r + 1) * cells_x // 8) * 8
    f32 = jnp.float32
    full = lambda planes: pltpu.VMEM((planes, ext, wide), f32)
    coarse = pltpu.VMEM((depth, rows_w, LANES), f32)
    dma = pltpu.SemaphoreType.DMA
    vmem = pl.BlockSpec(memory_space=pltpu.VMEM)
    anywhere = pl.BlockSpec(memory_space=pltpu.HBM)
    shape = jax.ShapeDtypeStruct(right_side.shape, f32)
    return pl.pallas_call(
        functools.partial(kernel, (nrow, ncol, reach_r, reach_c)),
        out_shape=(shape, shape),
        in_specs=[anywhere] * 5,
        out_specs=(vmem, vmem),
        scratch_shapes=[
            pltpu.SMEM(conductivity.shape, f32), pltpu.SMEM(capacity.shape, f32),
            pltpu.VMEM(right_side.shape, f32), pltpu.VMEM(guess.shape, f32),
            pltpu.VMEM(material.shape, jnp.int32), dma((5,)),
            full(depth + 2), full(depth + 2), full(depth + 2), full(depth), full(depth + 1),
            full(depth), full(depth), full(depth), full(depth), full(depth),
            pltpu.VMEM((2, depth, HALO, wy), f32),
            pltpu.VMEM((wx, LANES), f32), pltpu.VMEM((wx, LANES), f32),
            pltpu.VMEM((ext, LANES), f32), pltpu.VMEM((ext, LANES), f32),
            pltpu.VMEM((2, depth, HALO, wy), jnp.int32),
            pltpu.VMEM((3, wx, LANES), f32), pltpu.VMEM((3, wx, LANES), f32),
            pltpu.VMEM((3, ext, LANES), f32), pltpu.VMEM((3, ext, LANES), f32),
            pltpu.VMEM((2, ext, LANES), f32), pltpu.VMEM((2, ext, LANES), f32),
            pltpu.VMEM((2, depth, 8, wy), f32),
            pltpu.VMEM((2, cells_x, LANES), f32), pltpu.VMEM((1, cells_x, LANES), f32),
            pltpu.VMEM((2, 2 * reach_c + 1, rows_w, LANES), f32),
            pltpu.VMEM((1, 2 * reach_c + 1, rows_w, LANES), f32),
            coarse, coarse, coarse, coarse, coarse, coarse, coarse, coarse,
            dma((12,)), dma((12,)), dma((8,)), dma((8,)),
            dma((npeers,)), dma((npeers,)), dma((npeers,)), dma((npeers,)),
        ],
        compiler_params=pltpu.CompilerParams(
            collective_id=0, has_side_effects=True, vmem_limit_bytes=48 * 1024 * 1024
        ),
    )(conductivity, capacity, right_side, guess, material)


def solution(mesh):
    placed = (P(None, "row", "col"), P(None, "row", "col"), P(None, "row", "col"), P(), P())
    return jax.shard_map(
        functools.partial(shards, mesh.shape["row"], mesh.shape["col"]),
        mesh=mesh,
        in_specs=placed,
        out_specs=(P(None, "row", "col"), P(None, "row", "col")),
        check_vma=False,
    )
```

```python
import functools
import math

import jax
import jax.numpy as jnp
from jax import lax
from jax.experimental import pallas as pl
from jax.experimental.pallas import tpu as pltpu
from jax.sharding import PartitionSpec as P

COARSEN = 16
PRE = 2
POST = 2
CSWEEPS = 8
OMEGA = 0.8
HALO = 8
LANES = 128
HIGH = lax.Precision.HIGHEST
MESH = pl.DeviceIdType.MESH


def lane_ids(shape):
    return lax.broadcasted_iota(jnp.int32, shape, len(shape) - 1)


def row_ids(shape):
    return lax.broadcasted_iota(jnp.int32, shape, len(shape) - 2)


def kernel(
    sizes,
    cond_in, capa_in, rhs_in, guess_in, mat_in,
    out_ref, res_ref,
    cond_ref, capa_ref, rhs_ref, guess_ref, mat_ref, isem,
    va, vb, kap, cap, cz, cx, cy, rx, wgt, dia,
    uhalo, upack_l, upack_r, ur_l, ur_r, mhalo, pack_l, pack_r, recv_l, recv_r, kl, kr,
    xsum, tile_k, tile_r, grid_k, grid_r,
    hx, hy, hup, hinv, hgain, hback, hres, ecor,
    fsend, frecv, usend, urecv, ksend, krecv, rsend, rrecv,
):
    nrow, ncol, reach_r, reach_c = sizes
    depth, wx, wy = rhs_ref.shape
    ext = wx + 2 * HALO
    cells_x = wx // COARSEN
    cells_y = wy // COARSEN
    nclass = cond_ref.shape[0]
    row = lax.axis_index("row")
    col = lax.axis_index("col")
    rows_c = grid_r.shape[1]

    def exists(dr, dc):
        ok = (row + dr >= 0) & (row + dr < nrow)
        return ok & (col + dc >= 0) & (col + dc < ncol)

    def device(dr, dc):
        return (lax.rem(row + dr + nrow, nrow), lax.rem(col + dc + ncol, ncol))

    peers = [
        (dr, dc)
        for dr in range(-reach_r, reach_r + 1)
        for dc in range(-reach_c, reach_c + 1)
        if (dr, dc) != (0, 0)
    ]

    local = [
        pltpu.make_async_copy(src, dst, isem.at[index])
        for index, (src, dst) in enumerate((
            (guess_in, guess_ref), (rhs_in, rhs_ref), (mat_in, mat_ref),
            (cond_in, cond_ref), (capa_in, capa_ref),
        ))
    ]
    for copy in local:
        copy.start()
    uhalo[...] = jnp.zeros_like(uhalo)
    ur_l[...] = jnp.zeros_like(ur_l)
    ur_r[...] = jnp.zeros_like(ur_r)
    grid_k[...] = jnp.zeros_like(grid_k)
    grid_r[...] = jnp.zeros_like(grid_r)
    mhalo[...] = jnp.zeros_like(mhalo)
    recv_l[...] = jnp.zeros_like(recv_l)
    recv_r[...] = jnp.zeros_like(recv_r)
    lo, hi = slice(0, HALO), slice(ext - HALO, ext)
    own = slice(HALO, HALO + wx)
    for side in (lo, hi):
        va[1 : depth + 1, side, :wy] = jnp.zeros((depth, HALO, wy), jnp.float32)
        rx[:, side, :wy] = jnp.zeros((depth, HALO, wy), jnp.float32)

    barrier = pltpu.get_barrier_semaphore()
    for dr, dc in peers:
        @pl.when(exists(dr, dc))
        def _():
            pl.semaphore_signal(barrier, inc=1, device_id=device(dr, dc), device_id_type=MESH)

    lane = lane_ids((wx, LANES))

    def packed(plane_of):
        left = jnp.zeros((wx, LANES), jnp.float32)
        right = jnp.zeros((wx, LANES), jnp.float32)
        for z in range(depth):
            plane = plane_of(z)
            here = lane // 8 == z
            left = jnp.where(here, pltpu.roll(plane, (8 * z) % LANES, 1), left)
            right = jnp.where(here, pltpu.roll(plane, (8 * z + 8) % LANES, 1), right)
        return left, right

    for copy in local:
        copy.wait()
    for index, source in enumerate((guess_ref, rhs_ref, mat_ref)):
        left, right = packed(lambda z: source[z].astype(jnp.float32))
        pack_l[index] = left
        pack_r[index] = right

    tall_p = jnp.minimum(row + reach_r, nrow - 1) - jnp.maximum(row - reach_r, 0) + 1
    wide_p = jnp.minimum(col + reach_c, ncol - 1) - jnp.maximum(col - reach_c, 0) + 1
    pl.semaphore_wait(barrier, tall_p * wide_p - 1)

    zs = slice(1, depth + 1)

    def edge(dr, width):
        if dr == 1:
            return slice(wx - width, wx), slice(HALO - width, HALO)
        return slice(0, width), slice(HALO + wx, HALO + wx + width)

    def remote(plan, sends, recvs):
        copies = []
        for index, (dr, dc, src, dst) in enumerate(plan):
            copy = pltpu.make_async_remote_copy(
                src_ref=src, dst_ref=dst, send_sem=sends.at[index], recv_sem=recvs.at[index],
                device_id=device(dr, dc), device_id_type=MESH,
            )
            copies.append((dr, dc, copy))
        return copies

    def strips(packs, recvs, middle, wide_of):
        plan = []
        for dc, pack, recv in ((1, packs[1], recvs[0]), (-1, packs[0], recvs[1])):
            plan.append((0, dc, pack, recv.at[middle + (own,)]))
            for dr in (1, -1):
                src, dst = edge(dr, wide_of)
                plan.append((dr, dc, pack.at[middle + (src,)], recv.at[middle + (dst,)]))
        return plan

    near = PRE + 1
    plan = []
    for dr in (1, -1):
        src, dst = edge(dr, near)
        thin_src, thin_dst = edge(dr, near - 1)
        shift = 0 if dr == 1 else HALO + wx
        in_halo = slice(dst.start - shift, dst.stop - shift)
        plan.append((dr, 0, guess_ref.at[:, src, :], va.at[zs, dst, 0:wy]))
        plan.append((dr, 0, mat_ref.at[:, src, :], mhalo.at[0 if dr == 1 else 1, :, in_halo, :]))
        plan.append((dr, 0, rhs_ref.at[:, thin_src, :], rx.at[:, thin_dst, 0:wy]))
    plan += strips((pack_l, pack_r), (recv_l, recv_r), (slice(None),), near)
    fine = remote(plan, fsend, frecv)
    plan = []
    for dr in (1, -1):
        src, dst = edge(dr, POST + 1)
        shift = 0 if dr == 1 else HALO + wx
        src = slice(src.start + HALO, src.stop + HALO)
        in_halo = slice(dst.start - shift, dst.stop - shift)
        held = va if PRE % 2 == 0 else vb
        plan.append((dr, 0, held.at[zs, src, 0:wy], uhalo.at[0 if dr == 1 else 1, :, in_halo, :]))
    plan += strips((upack_l, upack_r), (ur_l, ur_r), (), POST + 1)
    pre_edges = remote(plan, usend, urecv)

    def start_all(copies):
        for dr, dc, copy in copies:
            @pl.when(exists(dr, dc))
            def _():
                copy.start()

    def recv_all(copies):
        for dr, dc, copy in copies:
            @pl.when(exists(-dr, -dc))
            def _():
                copy.wait_recv()

    def sent_all(copies):
        for dr, dc, copy in copies:
            @pl.when(exists(dr, dc))
            def _():
                copy.wait_send()

    start_all(fine)

    def lookup(classes):
        kval = jnp.full(classes.shape, cond_ref[0], jnp.float32)
        cval = jnp.full(classes.shape, capa_ref[0], jnp.float32)
        for k in range(1, nclass):
            hit = classes == k
            kval = jnp.where(hit, cond_ref[k], kval)
            cval = jnp.where(hit, capa_ref[k], cval)
        return kval, cval

    def xblocks(plane):
        part = plane.reshape(cells_x, COARSEN // 8, 8, wy).sum(axis=1)
        return part.sum(axis=1)

    xsum[...] = jnp.zeros_like(xsum)

    def own_fields(z, carry):
        kval, cval = lookup(mat_ref[z])
        kap[z + 1, own, 0:wy] = kval
        cap[z, own, 0:wy] = cval
        rx[z, own, 0:wy] = rhs_ref[z]
        va[z + 1, own, 0:wy] = guess_ref[z]
        xsum[0, z, 0:cells_x, :] = xblocks(kval)
        xsum[1, z, 0:cells_x, :] = xblocks(cval)
        return carry

    lax.fori_loop(0, depth, own_fields, 0)

    gather_rows = lax.broadcasted_iota(jnp.int32, (wy, LANES), 0) // COARSEN
    summing = (gather_rows == lane_ids((wy, LANES)) % cells_y).astype(jnp.float32)
    zshape = (depth, 8, LANES)
    zmask = lane_ids(zshape) // cells_y == lax.broadcasted_iota(jnp.int32, zshape, 0)

    def coarse_tile(which):
        block = jnp.dot(xsum[which].reshape(depth * 8, wy), summing, precision=HIGH,
                        preferred_element_type=jnp.float32)
        return jnp.where(zmask, block.reshape(zshape), 0.0).sum(axis=0)[0:cells_x]

    def spread(tile, grid, sends, recvs):
        copies = []
        for index, (dr, dc) in enumerate(peers):
            at = cells_x * (reach_r - dr)
            copy = pltpu.make_async_remote_copy(
                src_ref=tile, dst_ref=grid.at[:, reach_c - dc, at : at + cells_x, :],
                send_sem=sends.at[index], recv_sem=recvs.at[index],
                device_id=device(dr, dc), device_id_type=MESH,
            )
            copies.append((dr, dc, copy))
        return copies

    mid = slice(cells_x * reach_r, cells_x * (reach_r + 1))
    gk = grid_k
    tile_k[0] = coarse_tile(0) * (1.0 / (COARSEN * COARSEN))
    tile_k[1] = coarse_tile(1)
    spread_k = spread(tile_k, gk, ksend, krecv)
    start_all(spread_k)
    gk[0, reach_c, mid, :] = tile_k[0]
    gk[1, reach_c, mid, :] = tile_k[1]

    recv_all(fine)
    for field, side_ok in ((0, exists(-1, 0)), (1, exists(1, 0))):
        at = lo if field == 0 else hi
        kval, cval = lookup(mhalo[field])
        kap[zs, at, 0:wy] = jnp.where(side_ok, kval, 0.0)
        cap[:, at, 0:wy] = jnp.where(side_ok, cval, 0.0)
    prow = row_ids((ext, LANES))
    rows_ok = ((prow >= HALO) | (row > 0)) & ((prow < ext - HALO) | (row < nrow - 1))
    for recv, keep, side_ok in ((recv_l, kl, col > 0), (recv_r, kr, col < ncol - 1)):
        kval, cval = lookup(recv[2].astype(jnp.int32))
        ok = rows_ok & side_ok
        keep[0] = jnp.where(ok, kval, 0.0)
        keep[1] = jnp.where(ok, cval, 0.0)
    elane = lane_ids((ext, LANES))
    rim = slice(wy, wy + LANES)

    def unpack(lvals, rvals, dst, first_z):
        for z in range(depth):
            shift = (LANES - 8 * z) % LANES
            a = pltpu.roll(rvals, shift, 1) if shift else rvals
            shift = (LANES - 8 - 8 * z) % LANES
            b = pltpu.roll(lvals, shift, 1) if shift else lvals
            dst[z + first_z, :, rim] = jnp.where(elane < 8, a, jnp.where(elane >= LANES - 8, b, 0.0))

    for left, right, dst, first_z in (
        (kl.at[0], kr.at[0], kap, 1),
        (kl.at[1], kr.at[1], cap, 0),
        (recv_l.at[0], recv_r.at[0], va, 1),
        (recv_l.at[1], recv_r.at[1], rx, 0),
    ):
        unpack(left[...], right[...], dst, first_z)
    zero = jnp.zeros((ext, wy + LANES), jnp.float32)
    for field in (va, vb, kap):
        field[0] = zero
        field[depth + 1] = zero

    wide = wy + LANES

    def xnext(p):
        return pltpu.roll(p, ext - 1, 0)

    def xprev(p):
        return pltpu.roll(p, 1, 0)

    def ynext(p):
        return pltpu.roll(p, wide - 1, 1)

    def yprev(p):
        return pltpu.roll(p, 1, 1)

    cz[0] = 0.5 * kap[1]

    def coefs(z, carry):
        k = kap[z + 1]
        zc = 0.5 * (k + kap[z + 2])
        xc = 0.5 * (k + xnext(k))
        yc = 0.5 * (k + ynext(k))
        cz[z + 1] = zc
        cx[z] = xc
        cy[z] = yc
        d = cap[z] + zc
        d = d + cz[z]
        d = d + xc
        d = d + xprev(xc)
        d = d + yc
        d = d + yprev(yc)
        dia[z] = d
        wgt[z] = jnp.where(k > 0.0, OMEGA / d, 0.0)
        va[z + 1] = jnp.where(k > 0.0, va[z + 1], 0.0)
        return carry

    lax.fori_loop(0, depth, coefs, 0)

    def around(src, z, v):
        t = rx[z] + cz[z + 1] * src[z + 2]
        t = t + cz[z] * src[z]
        xc = cx[z]
        t = t + xc * xnext(v)
        t = t + xprev(xc * v)
        yc = cy[z]
        t = t + yc * ynext(v)
        return t + yprev(yc * v)

    def sweep(src, dst):
        def body(z, carry):
            v = src[z + 1]
            dst[z + 1] = (1.0 - OMEGA) * v + wgt[z] * around(src, z, v)
            return carry

        lax.fori_loop(0, depth, body, 0)

    def inner_residual(src, z):
        v = src[z + 1]
        return (around(src, z, v) - dia[z] * v)[own, 0:wy]

    bufs = [va, vb]
    for _ in range(PRE):
        sweep(bufs[0], bufs[1])
        bufs.reverse()

    def restrict(z, carry):
        xsum[0, z, 0:cells_x, :] = xblocks(inner_residual(bufs[0], z))
        return carry

    lax.fori_loop(0, depth, restrict, 0)
    tile_r[0] = coarse_tile(0)
    spread_r = spread(tile_r, grid_r, rsend, rrecv)
    start_all(spread_r)
    grid_r[0, reach_c, mid, :] = tile_r[0]
    upack_l[...], upack_r[...] = packed(lambda z: bufs[0][z + 1, own, 0:wy])
    start_all(pre_edges)

    recv_all(spread_k)
    rows_w = grid_r.shape[2]
    wlane = lane_ids((rows_w, LANES))
    wrow = row_ids((rows_w, LANES))
    ncells_c = 2 * reach_c + 1
    crow = wrow + (row - reach_r) * cells_x
    ccol = wlane + (col - reach_c) * cells_y
    inside = (crow >= 0) & (crow < nrow * cells_x) & (ccol >= 0) & (ccol < ncol * cells_y)
    inside = inside & (wrow < (2 * reach_r + 1) * cells_x) & (wlane < ncells_c * cells_y)

    def window(grid, which, z):
        acc = jnp.zeros((rows_w, LANES), jnp.float32)
        for block in range(ncells_c):
            shift = (cells_y * (block - z)) % LANES
            part = grid[which, block]
            part = pltpu.roll(part, shift, 1) if shift else part
            acc = jnp.where(wlane // cells_y == block, part, acc)
        return jnp.where(inside, acc, 0.0)

    kb = [window(gk, 0, z) for z in range(depth)]
    factor = 0.5 * COARSEN * COARSEN
    below = factor * kb[0]
    gain = None
    for z in range(depth):
        k = kb[z]
        above = factor * (k + kb[z + 1]) if z + 1 < depth else factor * k
        xc = 0.5 * (k + pltpu.roll(k, rows_w - 1, 0))
        yc = 0.5 * (k + pltpu.roll(k, LANES - 1, 1))
        xm = pltpu.roll(xc, 1, 0)
        ym = pltpu.roll(yc, 1, 1)
        d = window(gk, 1, z) + above
        d = d + below
        d = d + xc
        d = d + xm
        d = d + yc
        d = d + ym
        upper = above if z + 1 < depth else jnp.zeros_like(above)
        denom = d if z == 0 else d - below * gain
        inv = jnp.where(inside, 1.0 / denom, 0.0)
        gain = upper * inv
        hx[z] = xc
        hy[z] = yc
        hinv[z] = inv
        hgain[z] = gain
        hback[z] = below * inv if z else jnp.zeros_like(inv)
        below = above

    recv_all(spread_r)
    for z in range(depth):
        hres[z] = window(grid_r, 0, z)
        ecor[z] = jnp.zeros((rows_w, LANES), jnp.float32)

    def coarse_sweep(step, carry):
        head = None
        heads = []
        for z in range(depth):
            e = ecor[z]
            xc, yc = hx[z], hy[z]
            r = hres[z] + xc * pltpu.roll(e, rows_w - 1, 0)
            r = r + pltpu.roll(xc * e, 1, 0)
            r = r + yc * pltpu.roll(e, LANES - 1, 1)
            r = r + pltpu.roll(yc * e, 1, 1)
            r = r * hinv[z]
            head = r if z == 0 else r + hback[z] * head
            heads.append(head)
        value = heads[-1]
        ecor[depth - 1] = value
        for z in range(depth - 2, -1, -1):
            value = heads[z] + hgain[z] * value
            ecor[z] = value
        return carry

    lax.fori_loop(0, CSWEEPS, coarse_sweep, 0)

    recv_all(pre_edges)
    sent_all(pre_edges)
    bufs[0][zs, lo, 0:wy] = uhalo[0]
    bufs[0][zs, hi, 0:wy] = uhalo[1]
    unpack(ur_l[...], ur_r[...], bufs[0], 1)
    own_r = cells_x * reach_r
    low_r = (own_r - 1) // 8 * 8
    top_r = -(-(own_r + cells_x + 1) // 8) * 8
    ylane = lane_ids((LANES, wide))
    place = jnp.where(ylane < wy + LANES // 2, ylane // COARSEN, -1) + cells_y * reach_c
    picking = (lax.broadcasted_iota(jnp.int32, (LANES, wide), 0) == place).astype(jnp.float32)

    def prolong(z, carry):
        e = ecor[z, low_r:top_r, :]
        spread_y = jnp.dot(e, picking, precision=HIGH, preferred_element_type=jnp.float32)
        parts = []
        for cell in range(-1, cells_x + 1):
            at = own_r + cell - low_r
            tall = COARSEN if 0 <= cell < cells_x else HALO
            parts.append(jnp.broadcast_to(spread_y[at : at + 1, :], (tall, wide)))
        whole = jnp.concatenate(parts, axis=0)
        bufs[0][z + 1] = jnp.where(kap[z + 1] > 0.0, bufs[0][z + 1] + whole, 0.0)
        return carry

    lax.fori_loop(0, depth, prolong, 0)
    for _ in range(POST):
        sweep(bufs[0], bufs[1])
        bufs.reverse()

    def finish(z, carry):
        out_ref[z] = bufs[0][z + 1, own, 0:wy]
        res_ref[z] = inner_residual(bufs[0], z)
        return carry

    lax.fori_loop(0, depth, finish, 0)
    sent_all(fine)
    sent_all(spread_k)
    sent_all(spread_r)


def shards(nrow, ncol, right_side, guess, material, conductivity, capacity):
    depth, wx, wy = right_side.shape
    ext, wide = wx + 2 * HALO, wy + LANES
    cells_x, cells_y = wx // COARSEN, wy // COARSEN
    reach_r = min(math.ceil((CSWEEPS + 1) / cells_x), nrow - 1)
    reach_c = min(math.ceil((CSWEEPS + 1) / cells_y), ncol - 1)
    npeers = (2 * reach_r + 1) * (2 * reach_c + 1) - 1
    rows_w = -(-(2 * reach_r + 1) * cells_x // 8) * 8
    f32 = jnp.float32
    full = lambda planes: pltpu.VMEM((planes, ext, wide), f32)
    coarse = pltpu.VMEM((depth, rows_w, LANES), f32)
    dma = pltpu.SemaphoreType.DMA
    vmem = pl.BlockSpec(memory_space=pltpu.VMEM)
    anywhere = pl.BlockSpec(memory_space=pltpu.HBM)
    shape = jax.ShapeDtypeStruct(right_side.shape, f32)
    return pl.pallas_call(
        functools.partial(kernel, (nrow, ncol, reach_r, reach_c)),
        out_shape=(shape, shape),
        in_specs=[anywhere] * 5,
        out_specs=(vmem, vmem),
        scratch_shapes=[
            pltpu.SMEM(conductivity.shape, f32), pltpu.SMEM(capacity.shape, f32),
            pltpu.VMEM(right_side.shape, f32), pltpu.VMEM(guess.shape, f32),
            pltpu.VMEM(material.shape, jnp.int32), dma((5,)),
            full(depth + 2), full(depth + 2), full(depth + 2), full(depth), full(depth + 1),
            full(depth), full(depth), full(depth), full(depth), full(depth),
            pltpu.VMEM((2, depth, HALO, wy), f32),
            pltpu.VMEM((wx, LANES), f32), pltpu.VMEM((wx, LANES), f32),
            pltpu.VMEM((ext, LANES), f32), pltpu.VMEM((ext, LANES), f32),
            pltpu.VMEM((2, depth, HALO, wy), jnp.int32),
            pltpu.VMEM((3, wx, LANES), f32), pltpu.VMEM((3, wx, LANES), f32),
            pltpu.VMEM((3, ext, LANES), f32), pltpu.VMEM((3, ext, LANES), f32),
            pltpu.VMEM((2, ext, LANES), f32), pltpu.VMEM((2, ext, LANES), f32),
            pltpu.VMEM((2, depth, 8, wy), f32),
            pltpu.VMEM((2, cells_x, LANES), f32), pltpu.VMEM((1, cells_x, LANES), f32),
            pltpu.VMEM((2, 2 * reach_c + 1, rows_w, LANES), f32),
            pltpu.VMEM((1, 2 * reach_c + 1, rows_w, LANES), f32),
            coarse, coarse, coarse, coarse, coarse, coarse, coarse, coarse,
            dma((12,)), dma((12,)), dma((8,)), dma((8,)),
            dma((npeers,)), dma((npeers,)), dma((npeers,)), dma((npeers,)),
        ],
        compiler_params=pltpu.CompilerParams(
            collective_id=0, has_side_effects=True, vmem_limit_bytes=58 * 1024 * 1024
        ),
    )(conductivity, capacity, right_side, guess, material)


def solution(mesh):
    placed = (P(None, "row", "col"), P(None, "row", "col"), P(None, "row", "col"), P(), P())
    return jax.shard_map(
        functools.partial(shards, mesh.shape["row"], mesh.shape["col"]),
        mesh=mesh,
        in_specs=placed,
        out_specs=(P(None, "row", "col"), P(None, "row", "col")),
        check_vma=False,
    )
```

```python
import functools
import math

import jax
import jax.numpy as jnp
from jax import lax
from jax.experimental import pallas as pl
from jax.experimental.pallas import tpu as pltpu
from jax.sharding import PartitionSpec as P

COARSEN = 16
PRE = 2
POST = 2
CSWEEPS = 8
OMEGA = 0.8
HALO = 8
LANES = 128
HIGH = lax.Precision.HIGHEST
MESH = pl.DeviceIdType.MESH


def lane_ids(shape):
    return lax.broadcasted_iota(jnp.int32, shape, len(shape) - 1)


def row_ids(shape):
    return lax.broadcasted_iota(jnp.int32, shape, len(shape) - 2)


def kernel(
    sizes,
    cond_in, capa_in, rhs_in, guess_in, mat_in,
    out_hbm, res_hbm,
    res_ref, osem,
    cond_ref, capa_ref, rhs_ref, guess_ref, mat_ref, isem,
    va, vb, kap, cap, cz, cx, cy, rx, wgt, dia,
    uhalo, upack_l, upack_r, ur_l, ur_r, mhalo, pack_l, pack_r, recv_l, recv_r, kl, kr,
    xsum, tile_k, tile_r, grid_k, grid_r,
    hx, hy, hup, hinv, hgain, hback, hres, ecor,
    fsend, frecv, usend, urecv, ksend, krecv, rsend, rrecv,
):
    nrow, ncol, reach_r, reach_c = sizes
    depth, wx, wy = rhs_ref.shape
    ext = wx + 2 * HALO
    cells_x = wx // COARSEN
    cells_y = wy // COARSEN
    nclass = cond_ref.shape[0]
    row = lax.axis_index("row")
    col = lax.axis_index("col")
    rows_c = grid_r.shape[1]

    def exists(dr, dc):
        ok = (row + dr >= 0) & (row + dr < nrow)
        return ok & (col + dc >= 0) & (col + dc < ncol)

    def device(dr, dc):
        return (lax.rem(row + dr + nrow, nrow), lax.rem(col + dc + ncol, ncol))

    peers = [
        (dr, dc)
        for dr in range(-reach_r, reach_r + 1)
        for dc in range(-reach_c, reach_c + 1)
        if (dr, dc) != (0, 0)
    ]

    local = [
        pltpu.make_async_copy(src, dst, isem.at[index])
        for index, (src, dst) in enumerate((
            (guess_in, guess_ref), (rhs_in, rhs_ref), (mat_in, mat_ref),
            (cond_in, cond_ref), (capa_in, capa_ref),
        ))
    ]
    for copy in local:
        copy.start()
    uhalo[...] = jnp.zeros_like(uhalo)
    ur_l[...] = jnp.zeros_like(ur_l)
    ur_r[...] = jnp.zeros_like(ur_r)
    grid_k[...] = jnp.zeros_like(grid_k)
    grid_r[...] = jnp.zeros_like(grid_r)
    mhalo[...] = jnp.zeros_like(mhalo)
    recv_l[...] = jnp.zeros_like(recv_l)
    recv_r[...] = jnp.zeros_like(recv_r)
    lo, hi = slice(0, HALO), slice(ext - HALO, ext)
    own = slice(HALO, HALO + wx)
    for side in (lo, hi):
        va[1 : depth + 1, side, :wy] = jnp.zeros((depth, HALO, wy), jnp.float32)
        rx[:, side, :wy] = jnp.zeros((depth, HALO, wy), jnp.float32)

    barrier = pltpu.get_barrier_semaphore()
    for dr, dc in peers:
        @pl.when(exists(dr, dc))
        def _():
            pl.semaphore_signal(barrier, inc=1, device_id=device(dr, dc), device_id_type=MESH)

    lane = lane_ids((wx, LANES))

    def packed(plane_of):
        left = jnp.zeros((wx, LANES), jnp.float32)
        right = jnp.zeros((wx, LANES), jnp.float32)
        for z in range(depth):
            plane = plane_of(z)
            here = lane // 8 == z
            left = jnp.where(here, pltpu.roll(plane, (8 * z) % LANES, 1), left)
            right = jnp.where(here, pltpu.roll(plane, (8 * z + 8) % LANES, 1), right)
        return left, right

    for copy in local:
        copy.wait()
    for index, source in enumerate((guess_ref, rhs_ref, mat_ref)):
        left, right = packed(lambda z: source[z].astype(jnp.float32))
        pack_l[index] = left
        pack_r[index] = right

    tall_p = jnp.minimum(row + reach_r, nrow - 1) - jnp.maximum(row - reach_r, 0) + 1
    wide_p = jnp.minimum(col + reach_c, ncol - 1) - jnp.maximum(col - reach_c, 0) + 1
    pl.semaphore_wait(barrier, tall_p * wide_p - 1)

    zs = slice(1, depth + 1)

    def edge(dr, width):
        if dr == 1:
            return slice(wx - width, wx), slice(HALO - width, HALO)
        return slice(0, width), slice(HALO + wx, HALO + wx + width)

    def remote(plan, sends, recvs):
        copies = []
        for index, (dr, dc, src, dst) in enumerate(plan):
            copy = pltpu.make_async_remote_copy(
                src_ref=src, dst_ref=dst, send_sem=sends.at[index], recv_sem=recvs.at[index],
                device_id=device(dr, dc), device_id_type=MESH,
            )
            copies.append((dr, dc, copy))
        return copies

    def strips(packs, recvs, middle, wide_of):
        plan = []
        for dc, pack, recv in ((1, packs[1], recvs[0]), (-1, packs[0], recvs[1])):
            plan.append((0, dc, pack, recv.at[middle + (own,)]))
            for dr in (1, -1):
                src, dst = edge(dr, wide_of)
                plan.append((dr, dc, pack.at[middle + (src,)], recv.at[middle + (dst,)]))
        return plan

    near = PRE + 1
    plan = []
    for dr in (1, -1):
        src, dst = edge(dr, near)
        thin_src, thin_dst = edge(dr, near - 1)
        shift = 0 if dr == 1 else HALO + wx
        in_halo = slice(dst.start - shift, dst.stop - shift)
        plan.append((dr, 0, guess_ref.at[:, src, :], va.at[zs, dst, 0:wy]))
        plan.append((dr, 0, mat_ref.at[:, src, :], mhalo.at[0 if dr == 1 else 1, :, in_halo, :]))
        plan.append((dr, 0, rhs_ref.at[:, thin_src, :], rx.at[:, thin_dst, 0:wy]))
    plan += strips((pack_l, pack_r), (recv_l, recv_r), (slice(None),), near)
    fine = remote(plan, fsend, frecv)
    plan = []
    for dr in (1, -1):
        src, dst = edge(dr, POST + 1)
        shift = 0 if dr == 1 else HALO + wx
        src = slice(src.start + HALO, src.stop + HALO)
        in_halo = slice(dst.start - shift, dst.stop - shift)
        held = va if PRE % 2 == 0 else vb
        plan.append((dr, 0, held.at[zs, src, 0:wy], uhalo.at[0 if dr == 1 else 1, :, in_halo, :]))
    plan += strips((upack_l, upack_r), (ur_l, ur_r), (), POST + 1)
    pre_edges = remote(plan, usend, urecv)

    def start_all(copies):
        for dr, dc, copy in copies:
            @pl.when(exists(dr, dc))
            def _():
                copy.start()

    def recv_all(copies):
        for dr, dc, copy in copies:
            @pl.when(exists(-dr, -dc))
            def _():
                copy.wait_recv()

    def sent_all(copies):
        for dr, dc, copy in copies:
            @pl.when(exists(dr, dc))
            def _():
                copy.wait_send()

    start_all(fine)

    def lookup(classes):
        kval = jnp.full(classes.shape, cond_ref[0], jnp.float32)
        cval = jnp.full(classes.shape, capa_ref[0], jnp.float32)
        for k in range(1, nclass):
            hit = classes == k
            kval = jnp.where(hit, cond_ref[k], kval)
            cval = jnp.where(hit, capa_ref[k], cval)
        return kval, cval

    def xblocks(plane):
        part = plane.reshape(cells_x, COARSEN // 8, 8, wy).sum(axis=1)
        return part.sum(axis=1)

    xsum[...] = jnp.zeros_like(xsum)

    def own_fields(z, carry):
        kval, cval = lookup(mat_ref[z])
        kap[z + 1, own, 0:wy] = kval
        cap[z, own, 0:wy] = cval
        rx[z, own, 0:wy] = rhs_ref[z]
        va[z + 1, own, 0:wy] = guess_ref[z]
        xsum[0, z, 0:cells_x, :] = xblocks(kval)
        xsum[1, z, 0:cells_x, :] = xblocks(cval)
        return carry

    lax.fori_loop(0, depth, own_fields, 0)

    gather_rows = lax.broadcasted_iota(jnp.int32, (wy, LANES), 0) // COARSEN
    summing = (gather_rows == lane_ids((wy, LANES)) % cells_y).astype(jnp.float32)
    zshape = (depth, 8, LANES)
    zmask = lane_ids(zshape) // cells_y == lax.broadcasted_iota(jnp.int32, zshape, 0)

    def coarse_tile(which):
        block = jnp.dot(xsum[which].reshape(depth * 8, wy), summing, precision=HIGH,
                        preferred_element_type=jnp.float32)
        return jnp.where(zmask, block.reshape(zshape), 0.0).sum(axis=0)[0:cells_x]

    def spread(tile, grid, sends, recvs):
        copies = []
        for index, (dr, dc) in enumerate(peers):
            at = cells_x * (reach_r - dr)
            copy = pltpu.make_async_remote_copy(
                src_ref=tile, dst_ref=grid.at[:, reach_c - dc, at : at + cells_x, :],
                send_sem=sends.at[index], recv_sem=recvs.at[index],
                device_id=device(dr, dc), device_id_type=MESH,
            )
            copies.append((dr, dc, copy))
        return copies

    mid = slice(cells_x * reach_r, cells_x * (reach_r + 1))
    gk = grid_k
    tile_k[0] = coarse_tile(0) * (1.0 / (COARSEN * COARSEN))
    tile_k[1] = coarse_tile(1)
    spread_k = spread(tile_k, gk, ksend, krecv)
    start_all(spread_k)
    gk[0, reach_c, mid, :] = tile_k[0]
    gk[1, reach_c, mid, :] = tile_k[1]

    recv_all(fine)
    for field, side_ok in ((0, exists(-1, 0)), (1, exists(1, 0))):
        at = lo if field == 0 else hi
        kval, cval = lookup(mhalo[field])
        kap[zs, at, 0:wy] = jnp.where(side_ok, kval, 0.0)
        cap[:, at, 0:wy] = jnp.where(side_ok, cval, 0.0)
    prow = row_ids((ext, LANES))
    rows_ok = ((prow >= HALO) | (row > 0)) & ((prow < ext - HALO) | (row < nrow - 1))
    for recv, keep, side_ok in ((recv_l, kl, col > 0), (recv_r, kr, col < ncol - 1)):
        kval, cval = lookup(recv[2].astype(jnp.int32))
        ok = rows_ok & side_ok
        keep[0] = jnp.where(ok, kval, 0.0)
        keep[1] = jnp.where(ok, cval, 0.0)
    elane = lane_ids((ext, LANES))
    rim = slice(wy, wy + LANES)

    def unpack(lvals, rvals, dst, first_z):
        for z in range(depth):
            shift = (LANES - 8 * z) % LANES
            a = pltpu.roll(rvals, shift, 1) if shift else rvals
            shift = (LANES - 8 - 8 * z) % LANES
            b = pltpu.roll(lvals, shift, 1) if shift else lvals
            dst[z + first_z, :, rim] = jnp.where(elane < 8, a, jnp.where(elane >= LANES - 8, b, 0.0))

    for left, right, dst, first_z in (
        (kl.at[0], kr.at[0], kap, 1),
        (kl.at[1], kr.at[1], cap, 0),
        (recv_l.at[0], recv_r.at[0], va, 1),
        (recv_l.at[1], recv_r.at[1], rx, 0),
    ):
        unpack(left[...], right[...], dst, first_z)
    zero = jnp.zeros((ext, wy + LANES), jnp.float32)
    for field in (va, vb, kap):
        field[0] = zero
        field[depth + 1] = zero

    wide = wy + LANES

    def xnext(p):
        return pltpu.roll(p, ext - 1, 0)

    def xprev(p):
        return pltpu.roll(p, 1, 0)

    def ynext(p):
        return pltpu.roll(p, wide - 1, 1)

    def yprev(p):
        return pltpu.roll(p, 1, 1)

    cz[0] = 0.5 * kap[1]

    def coefs(z, carry):
        k = kap[z + 1]
        zc = 0.5 * (k + kap[z + 2])
        xc = 0.5 * (k + xnext(k))
        yc = 0.5 * (k + ynext(k))
        cz[z + 1] = zc
        cx[z] = xc
        cy[z] = yc
        d = cap[z] + zc
        d = d + cz[z]
        d = d + xc
        d = d + xprev(xc)
        d = d + yc
        d = d + yprev(yc)
        dia[z] = d
        wgt[z] = jnp.where(k > 0.0, OMEGA / d, 0.0)
        va[z + 1] = jnp.where(k > 0.0, va[z + 1], 0.0)
        return carry

    lax.fori_loop(0, depth, coefs, 0)

    def around(src, z, v):
        t = rx[z] + cz[z + 1] * src[z + 2]
        t = t + cz[z] * src[z]
        xc = cx[z]
        t = t + xc * xnext(v)
        t = t + xprev(xc * v)
        yc = cy[z]
        t = t + yc * ynext(v)
        return t + yprev(yc * v)

    def sweep(src, dst):
        def body(z, carry):
            v = src[z + 1]
            dst[z + 1] = (1.0 - OMEGA) * v + wgt[z] * around(src, z, v)
            return carry

        lax.fori_loop(0, depth, body, 0)

    def inner_residual(src, z):
        v = src[z + 1]
        return (around(src, z, v) - dia[z] * v)[own, 0:wy]

    bufs = [va, vb]
    for _ in range(PRE):
        sweep(bufs[0], bufs[1])
        bufs.reverse()

    def restrict(z, carry):
        xsum[0, z, 0:cells_x, :] = xblocks(inner_residual(bufs[0], z))
        return carry

    lax.fori_loop(0, depth, restrict, 0)
    tile_r[0] = coarse_tile(0)
    spread_r = spread(tile_r, grid_r, rsend, rrecv)
    start_all(spread_r)
    grid_r[0, reach_c, mid, :] = tile_r[0]
    upack_l[...], upack_r[...] = packed(lambda z: bufs[0][z + 1, own, 0:wy])
    start_all(pre_edges)

    recv_all(spread_k)
    rows_w = grid_r.shape[2]
    wlane = lane_ids((rows_w, LANES))
    wrow = row_ids((rows_w, LANES))
    ncells_c = 2 * reach_c + 1
    crow = wrow + (row - reach_r) * cells_x
    ccol = wlane + (col - reach_c) * cells_y
    inside = (crow >= 0) & (crow < nrow * cells_x) & (ccol >= 0) & (ccol < ncol * cells_y)
    inside = inside & (wrow < (2 * reach_r + 1) * cells_x) & (wlane < ncells_c * cells_y)

    def window(grid, which, z):
        acc = jnp.zeros((rows_w, LANES), jnp.float32)
        for block in range(ncells_c):
            shift = (cells_y * (block - z)) % LANES
            part = grid[which, block]
            part = pltpu.roll(part, shift, 1) if shift else part
            acc = jnp.where(wlane // cells_y == block, part, acc)
        return jnp.where(inside, acc, 0.0)

    kb = [window(gk, 0, z) for z in range(depth)]
    factor = 0.5 * COARSEN * COARSEN
    below = factor * kb[0]
    gain = None
    for z in range(depth):
        k = kb[z]
        above = factor * (k + kb[z + 1]) if z + 1 < depth else factor * k
        xc = 0.5 * (k + pltpu.roll(k, rows_w - 1, 0))
        yc = 0.5 * (k + pltpu.roll(k, LANES - 1, 1))
        xm = pltpu.roll(xc, 1, 0)
        ym = pltpu.roll(yc, 1, 1)
        d = window(gk, 1, z) + above
        d = d + below
        d = d + xc
        d = d + xm
        d = d + yc
        d = d + ym
        upper = above if z + 1 < depth else jnp.zeros_like(above)
        denom = d if z == 0 else d - below * gain
        inv = jnp.where(inside, 1.0 / denom, 0.0)
        gain = upper * inv
        hx[z] = xc
        hy[z] = yc
        hinv[z] = inv
        hgain[z] = gain
        hback[z] = below * inv if z else jnp.zeros_like(inv)
        below = above

    recv_all(spread_r)
    for z in range(depth):
        hres[z] = window(grid_r, 0, z)
        ecor[z] = jnp.zeros((rows_w, LANES), jnp.float32)

    def coarse_sweep(step, carry):
        head = None
        heads = []
        for z in range(depth):
            e = ecor[z]
            xc, yc = hx[z], hy[z]
            r = hres[z] + xc * pltpu.roll(e, rows_w - 1, 0)
            r = r + pltpu.roll(xc * e, 1, 0)
            r = r + yc * pltpu.roll(e, LANES - 1, 1)
            r = r + pltpu.roll(yc * e, 1, 1)
            r = r * hinv[z]
            head = r if z == 0 else r + hback[z] * head
            heads.append(head)
        value = heads[-1]
        ecor[depth - 1] = value
        for z in range(depth - 2, -1, -1):
            value = heads[z] + hgain[z] * value
            ecor[z] = value
        return carry

    lax.fori_loop(0, CSWEEPS, coarse_sweep, 0)

    recv_all(pre_edges)
    sent_all(pre_edges)
    bufs[0][zs, lo, 0:wy] = uhalo[0]
    bufs[0][zs, hi, 0:wy] = uhalo[1]
    unpack(ur_l[...], ur_r[...], bufs[0], 1)
    own_r = cells_x * reach_r
    low_r = (own_r - 1) // 8 * 8
    top_r = -(-(own_r + cells_x + 1) // 8) * 8
    ylane = lane_ids((LANES, wide))
    place = jnp.where(ylane < wy + LANES // 2, ylane // COARSEN, -1) + cells_y * reach_c
    picking = (lax.broadcasted_iota(jnp.int32, (LANES, wide), 0) == place).astype(jnp.float32)

    def prolong(z, carry):
        e = ecor[z, low_r:top_r, :]
        spread_y = jnp.dot(e, picking, precision=HIGH, preferred_element_type=jnp.float32)
        parts = []
        for cell in range(-1, cells_x + 1):
            at = own_r + cell - low_r
            tall = COARSEN if 0 <= cell < cells_x else HALO
            parts.append(jnp.broadcast_to(spread_y[at : at + 1, :], (tall, wide)))
        whole = jnp.concatenate(parts, axis=0)
        bufs[0][z + 1] = jnp.where(kap[z + 1] > 0.0, bufs[0][z + 1] + whole, 0.0)
        return carry

    lax.fori_loop(0, depth, prolong, 0)
    for _ in range(POST):
        sweep(bufs[0], bufs[1])
        bufs.reverse()

    outs = [pltpu.make_async_copy(bufs[0].at[zs, own, 0:wy], out_hbm, osem.at[0])]
    outs[0].start()

    def finish(z, carry):
        res_ref[z] = inner_residual(bufs[0], z)
        return carry

    half = depth // 2
    for index, part in ((1, (0, half)), (2, (half, depth))):
        lax.fori_loop(part[0], part[1], finish, 0)
        planes = slice(part[0], part[1])
        outs.append(pltpu.make_async_copy(res_ref.at[planes], res_hbm.at[planes], osem.at[index]))
        outs[-1].start()
    sent_all(fine)
    sent_all(spread_k)
    sent_all(spread_r)
    for copy in outs:
        copy.wait()


def shards(nrow, ncol, right_side, guess, material, conductivity, capacity):
    depth, wx, wy = right_side.shape
    ext, wide = wx + 2 * HALO, wy + LANES
    cells_x, cells_y = wx // COARSEN, wy // COARSEN
    reach_r = min(math.ceil((CSWEEPS + 1) / cells_x), nrow - 1)
    reach_c = min(math.ceil((CSWEEPS + 1) / cells_y), ncol - 1)
    npeers = (2 * reach_r + 1) * (2 * reach_c + 1) - 1
    rows_w = -(-(2 * reach_r + 1) * cells_x // 8) * 8
    f32 = jnp.float32
    full = lambda planes: pltpu.VMEM((planes, ext, wide), f32)
    coarse = pltpu.VMEM((depth, rows_w, LANES), f32)
    dma = pltpu.SemaphoreType.DMA
    anywhere = pl.BlockSpec(memory_space=pltpu.HBM)
    shape = jax.ShapeDtypeStruct(right_side.shape, f32)
    return pl.pallas_call(
        functools.partial(kernel, (nrow, ncol, reach_r, reach_c)),
        out_shape=(shape, shape),
        in_specs=[anywhere] * 5,
        out_specs=(anywhere, anywhere),
        scratch_shapes=[
            pltpu.VMEM(right_side.shape, f32), dma((3,)),
            pltpu.SMEM(conductivity.shape, f32), pltpu.SMEM(capacity.shape, f32),
            pltpu.VMEM(right_side.shape, f32), pltpu.VMEM(guess.shape, f32),
            pltpu.VMEM(material.shape, jnp.int32), dma((5,)),
            full(depth + 2), full(depth + 2), full(depth + 2), full(depth), full(depth + 1),
            full(depth), full(depth), full(depth), full(depth), full(depth),
            pltpu.VMEM((2, depth, HALO, wy), f32),
            pltpu.VMEM((wx, LANES), f32), pltpu.VMEM((wx, LANES), f32),
            pltpu.VMEM((ext, LANES), f32), pltpu.VMEM((ext, LANES), f32),
            pltpu.VMEM((2, depth, HALO, wy), jnp.int32),
            pltpu.VMEM((3, wx, LANES), f32), pltpu.VMEM((3, wx, LANES), f32),
            pltpu.VMEM((3, ext, LANES), f32), pltpu.VMEM((3, ext, LANES), f32),
            pltpu.VMEM((2, ext, LANES), f32), pltpu.VMEM((2, ext, LANES), f32),
            pltpu.VMEM((2, depth, 8, wy), f32),
            pltpu.VMEM((2, cells_x, LANES), f32), pltpu.VMEM((1, cells_x, LANES), f32),
            pltpu.VMEM((2, 2 * reach_c + 1, rows_w, LANES), f32),
            pltpu.VMEM((1, 2 * reach_c + 1, rows_w, LANES), f32),
            coarse, coarse, coarse, coarse, coarse, coarse, coarse, coarse,
            dma((12,)), dma((12,)), dma((8,)), dma((8,)),
            dma((npeers,)), dma((npeers,)), dma((npeers,)), dma((npeers,)),
        ],
        compiler_params=pltpu.CompilerParams(
            collective_id=0, has_side_effects=True, vmem_limit_bytes=58 * 1024 * 1024
        ),
    )(conductivity, capacity, right_side, guess, material)


def solution(mesh):
    placed = (P(None, "row", "col"), P(None, "row", "col"), P(None, "row", "col"), P(), P())
    return jax.shard_map(
        functools.partial(shards, mesh.shape["row"], mesh.shape["col"]),
        mesh=mesh,
        in_specs=placed,
        out_specs=(P(None, "row", "col"), P(None, "row", "col")),
        check_vma=False,
    )
```
